512 devices in a mesh: aa: 32 (over y, x), ba: 16 (over z, core).
Axes of the slice: x: 4, y: 8, z: 8, core: 2. Of those that a mesh axis runs over, the one named last changes fastest.
Arguments:
- feat_a: bfloat16 [16384, 256], P(('aa', 'ba')), may hold values from -32 to 32
- feat_b: bfloat16 [65536, 256], P(('ba', 'aa')), may hold values from -32 to 32
- col_max_other: float32 [65536], P('ba'), may hold values from 1 to 3
- col_sum_other: float32 [65536], P('ba'), may hold values from 5734.4 to 114688
Outputs:
- confidence: bfloat16 [16384, 65536], P('aa', 'ba')
The draws below stay inside these ranges and needn't reach their ends.
All inputs are finite; a program needn't handle non-finite values.
Results may differ from the reference program's by a relative error of at most 0.0034.
Values may be sent and summed in bfloat16 or wider, within the bound.
No kernel may reach another device: no remote copies, remote signals or barrier semaphores. Data moves between devices by JAX's collectives and lax.ppermute only.
A program may use at most 64 MiB of HBM per device.

```python
import math
import jax
import jax.numpy as jnp
from jax import lax

C = 256
A_DEV = 512
FRAME_A = 131072
LA = 16384
NB = 65536


def draw_feat_a(key, part):
    key = jax.random.fold_in(key, 11)
    return jnp.clip(jax.random.normal(key, (LA, C), jnp.float32), -6.0, 6.0).astype(jnp.bfloat16)


def draw_feat_b(key, part):
    key = jax.random.fold_in(key, 23)
    return jnp.clip(jax.random.normal(key, (NB, C), jnp.float32), -6.0, 6.0).astype(jnp.bfloat16)


def block_levels(key, shape, cuts, least, high):
    level = 1.0
    for dim, parts in cuts:
        heights = jax.random.uniform(jax.random.fold_in(jax.random.fold_in(key, 6), dim), (parts,), jnp.float32, least / len(cuts), high / len(cuts))
        level = level * jnp.repeat(jnp.exp(heights), shape[dim] // parts).reshape((-1,) + (1,) * (len(shape) - 1 - dim))
    return level


def setup_inputs(seed: int = 0) -> dict:
    keys = jax.random.split(jax.random.key(seed), 5)
    feat_a = draw_feat_a(jax.random.fold_in(keys[4], 71), 0)
    feat_b = draw_feat_b(jax.random.fold_in(keys[4], 71), 0)
    col_max_other = jnp.clip(1.0 + 2.0 * jax.random.uniform(keys[2], (NB,), jnp.float32) ** block_levels(keys[2], (NB,), ((0, 16),), -0.2, 0.2), 1.0, 3.0)
    col_sum_other = jnp.clip(jnp.exp(math.log(114688.0) - 2.9957323 * jax.random.uniform(keys[3], (NB,), jnp.float32) ** block_levels(keys[3], (NB,), ((0, 16),), -0.2, 0.2)), 5734.4, 114688.0)
    return {"feat_a": feat_a, "feat_b": feat_b, "col_max_other": col_max_other, "col_sum_other": col_sum_other}


temper = 0.1


def score_block(slab_rows, feat_b):
    return jnp.dot(slab_rows, feat_b.T, preferred_element_type=jnp.float32) * (1.0 / (C * temper))


def reference(feat_a, feat_b, col_max_other, col_sum_other):
    blocks = feat_a.reshape(LA // A_DEV, A_DEV, C)

    def statistics(slab_rows):
        tile_scores = score_block(slab_rows, feat_b)
        row_top = jnp.max(tile_scores, axis=1)
        row_tot = jnp.sum(jnp.exp(tile_scores - row_top[:, None]), axis=1)
        col_top = jnp.max(tile_scores, axis=0)
        col_tot = jnp.sum(jnp.exp(tile_scores - col_top[None, :]), axis=0)
        return row_top, row_tot, col_top, col_tot

    row_top, row_tot, col_top, col_tot = lax.map(statistics, blocks)
    col_max = jnp.maximum(jnp.max(col_top, axis=0), col_max_other)
    col_sum = jnp.sum(col_tot * jnp.exp(col_top - col_max[None, :]), axis=0)
    col_sum = col_sum + col_sum_other * jnp.exp(col_max_other - col_max)
    scale_up = float(FRAME_A) * float(NB)

    def finish(packed):
        slab_rows, row_max, row_sum = packed
        tile_scores = score_block(slab_rows, feat_b)
        row_part = jnp.exp(tile_scores - row_max[:, None]) / row_sum[:, None]
        col_part = jnp.exp(tile_scores - col_max[None, :]) / col_sum[None, :]
        return (row_part * col_part * scale_up).astype(jnp.bfloat16)

    result = lax.map(finish, (blocks, row_top, row_tot))
    return result.reshape(LA, NB)
```

```python
import functools
import math

import jax
import jax.numpy as jnp
from jax import lax
from jax.experimental import pallas as pl
from jax.experimental.pallas import tpu as pltpu
from jax.sharding import Mesh
from jax.sharding import PartitionSpec as P

FRAME_A = 131072
TEMPER = 0.1
LOG2E = math.log2(math.e)
AA = ("y", "x")
BA = ("z", "core")


def spread(block, axis):
    n = lax.axis_size(axis)
    return lax.all_to_all(jnp.broadcast_to(block[None], (n,) + block.shape), axis, 0, 0, tiled=True)


def block_scores(a_ref, b_ref, j, factor):
    b = b_ref[:, j].reshape(-1, b_ref.shape[-1])
    d = lax.dot_general(a_ref[...], b, (((1,), (1,)), ((), ())), preferred_element_type=jnp.float32)
    return d * (factor * LOG2E)


def stats_kernel(factor, a_ref, b_ref, row_ref, col_ref, s_ref):
    rows, columns = a_ref.shape[0], col_ref.shape[1]
    blocks = b_ref.shape[1]
    width = columns // blocks
    lanes = 128

    def first(j, top):
        s = block_scores(a_ref, b_ref, j, factor)
        at = pl.ds(pl.multiple_of(j * width, width), width)
        s_ref[:, at] = s
        col_top = jnp.max(s, axis=0, keepdims=True)
        col_tot = jnp.sum(jnp.exp2(s - col_top), axis=0, keepdims=True)
        col_ref[:, at] = col_top + jnp.log2(col_tot)
        for c in range(0, width, lanes):
            top = jnp.maximum(top, s[:, c : c + lanes])
        return top

    top = lax.fori_loop(0, blocks, first, jnp.full((rows, lanes), -jnp.inf, jnp.float32))
    row_top = jnp.max(top, axis=1, keepdims=True)

    def second(j, tot):
        at = pl.ds(pl.multiple_of(j * width, width), width)
        e = jnp.exp2(s_ref[:, at] - row_top)
        for c in range(0, width, lanes):
            tot = tot + e[:, c : c + lanes]
        return tot

    tot = lax.fori_loop(0, blocks, second, jnp.zeros((rows, lanes), jnp.float32))
    lse = row_top + jnp.log2(jnp.sum(tot, axis=1, keepdims=True))
    row_ref[...] = jnp.broadcast_to(lse, (rows, lanes)).T[:1]


def stats(a, b, factor):
    rows = a.shape[0]
    columns = b.shape[0] * b.shape[1] * b.shape[2]
    vmem = pl.BlockSpec(memory_space=pltpu.VMEM)
    return pl.pallas_call(
        functools.partial(stats_kernel, factor),
        out_shape=(
            jax.ShapeDtypeStruct((1, rows), jnp.float32),
            jax.ShapeDtypeStruct((1, columns), jnp.float32),
        ),
        in_specs=[vmem, vmem],
        out_specs=(vmem, vmem),
        scratch_shapes=[pltpu.VMEM((rows, columns), jnp.float32)],
        compiler_params=pltpu.CompilerParams(vmem_limit_bytes=40 << 20),
        name="tile_statistics",
    )(a, b)


def finish_kernel(factor, shift, a_ref, b_ref, rows_ref, cols_ref, top_ref, tot_ref, out_ref, row_lse):
    j = pl.program_id(0)

    @pl.when(j == 0)
    def _():
        parts = rows_ref[:, 0]
        top = jnp.max(parts, axis=0, keepdims=True)
        lse = top + jnp.log2(jnp.sum(jnp.exp2(parts - top), axis=0, keepdims=True))
        row_lse[...] = jnp.broadcast_to(lse, (128, lse.shape[1])).T

    parts = cols_ref[:, 0]
    other_top = top_ref[...] * LOG2E
    top = jnp.maximum(jnp.max(parts, axis=0, keepdims=True), other_top)
    tot = jnp.sum(jnp.exp2(parts - top), axis=0, keepdims=True) + tot_ref[...] * jnp.exp2(other_top - top)
    col_lse = top + jnp.log2(tot) - shift
    s = block_scores(a_ref, b_ref, 0, factor)
    out_ref[...] = jnp.exp2((s - row_lse[:, :1]) + (s - col_lse)).astype(out_ref.dtype)


def finish(a, b, row_parts, col_parts, col_max_other, col_sum_other, factor, shift):
    rows = a.shape[0]
    nx, ny, n, c = b.shape
    columns = nx * ny * n
    width = nx * n
    na, nb = col_parts.shape[0], row_parts.shape[0]
    return pl.pallas_call(
        functools.partial(finish_kernel, factor, shift),
        out_shape=jax.ShapeDtypeStruct((rows, columns), jnp.bfloat16),
        grid=(ny,),
        in_specs=[
            pl.BlockSpec((rows, c), lambda j: (0, 0)),
            pl.BlockSpec((nx, 1, n, c), lambda j: (0, j, 0, 0)),
            pl.BlockSpec((nb, 1, rows), lambda j: (0, 0, 0)),
            pl.BlockSpec((na, 1, width), lambda j: (0, 0, j)),
            pl.BlockSpec((1, width), lambda j: (0, j)),
            pl.BlockSpec((1, width), lambda j: (0, j)),
        ],
        out_specs=pl.BlockSpec((rows, width), lambda j: (0, j)),
        scratch_shapes=[pltpu.VMEM((rows, 128), jnp.float32)],
        compiler_params=pltpu.CompilerParams(vmem_limit_bytes=40 << 20),
        name="confidence",
    )(a, b, row_parts, col_parts, col_max_other[None], col_sum_other[None])


def local(feat_a, feat_b, col_max_other, col_sum_other):
    factor = 1.0 / (feat_a.shape[1] * TEMPER)
    columns = feat_b.shape[0] * lax.axis_size(AA)
    shift = math.log2(float(FRAME_A) * float(columns * lax.axis_size(BA)))
    a = spread(feat_a, BA).reshape(-1, feat_a.shape[1])
    b = spread(spread(feat_b, "y"), "x")
    row_lse, col_lse = stats(a, b, factor)
    row_parts = spread(row_lse, BA)
    col_parts = spread(col_lse, AA)
    return finish(a, b, row_parts, col_parts, col_max_other, col_sum_other, factor, shift)


def solution(mesh):
    inner = Mesh(mesh.devices.reshape(8, 4, 8, 2), AA + BA)
    in_specs = (P(AA + BA, None), P(BA + AA, None), P(BA), P(BA))
    out_specs = P(AA, BA)
    return jax.shard_map(local, mesh=inner, in_specs=in_specs, out_specs=out_specs, check_vma=False)
```

```python
import functools
import math

import jax
import jax.numpy as jnp
from jax import lax
from jax.experimental import pallas as pl
from jax.experimental.pallas import tpu as pltpu
from jax.sharding import Mesh
from jax.sharding import PartitionSpec as P

FRAME_A = 131072
TEMPER = 0.1
LOG2E = math.log2(math.e)
AA = ("y", "x")
BA = ("z", "core")
LANES = 128
WIDTH = 256
SAFE_LOW, SAFE_HIGH = 2.0**-40, 2.0**100
VMEM_LIMIT = 48 << 20


def spread(block, axis):
    n = lax.axis_size(axis)
    return lax.all_to_all(jnp.broadcast_to(block[None], (n,) + block.shape), axis, 0, 0, tiled=True)


def scores(a, b, scale):
    return lax.dot_general(a, b, (((1,), (1,)), ((), ())), preferred_element_type=jnp.float32) * scale


def to_lanes(column):
    return jnp.sum(column.T, axis=0, keepdims=True)


def lse_over(parts, axis):
    top = jnp.max(parts, axis=axis, keepdims=True)
    return jnp.squeeze(top + jnp.log2(jnp.sum(jnp.exp2(parts - top), axis=axis, keepdims=True)), axis)


def part_statistics(scale, a_ref, b_refs, row_ref, col_ref):
    rows = a_ref.shape[0]
    blocks, n, c = b_refs[0].shape
    per = WIDTH // n
    work = [(ref, i) for ref in b_refs for i in range(0, blocks, per)]

    def put_col(t, lse):
        for k in range(per):
            col_ref[pl.ds(t * per + k, 1), :] = lse[:, k * LANES : (k + 1) * LANES]

    def put_row(lse):
        for k in range(rows // LANES):
            row_ref[pl.ds(k, 1), :] = lse[:, k * LANES : (k + 1) * LANES]

    tot = jnp.zeros((rows, LANES), jnp.float32)
    for t, (ref, i) in enumerate(work):
        e = jnp.exp2(scores(a_ref[...], ref[i : i + per].reshape(WIDTH, c), scale))
        put_col(t, jnp.log2(jnp.sum(e, axis=0, keepdims=True)))
        for k in range(per):
            tot = tot + e[:, k * LANES : (k + 1) * LANES]
    row_tot = to_lanes(tot)
    put_row(jnp.log2(row_tot))
    in_range = (jnp.min(row_tot) > SAFE_LOW) & (jnp.max(row_tot) < SAFE_HIGH)

    @pl.when(jnp.logical_not(in_range))
    def _():
        top = jnp.full((rows, 1), -jnp.inf, jnp.float32)
        for t, (ref, i) in enumerate(work):
            s = scores(a_ref[...], ref[i : i + per].reshape(WIDTH, c), scale)
            col_top = jnp.max(s, axis=0, keepdims=True)
            put_col(t, col_top + jnp.log2(jnp.sum(jnp.exp2(s - col_top), axis=0, keepdims=True)))
            top = jnp.maximum(top, jnp.max(s, axis=1, keepdims=True))
        tot = jnp.zeros((rows, LANES), jnp.float32)
        for ref, i in work:
            e = jnp.exp2(scores(a_ref[...], ref[i : i + per].reshape(WIDTH, c), scale) - top)
            for k in range(per):
                tot = tot + e[:, k * LANES : (k + 1) * LANES]
        row_top = jnp.broadcast_to(top, (rows, LANES)).T[:1]
        put_row(row_top + jnp.log2(to_lanes(tot)))


def early_kernel(scale, a_ref, *refs):
    part_statistics(scale, a_ref, refs[:-2], *refs[-2:])


def early_statistics(a, parts, scale):
    rows = a.shape[0]
    blocks = sum(p.shape[0] for p in parts)
    vmem = pl.BlockSpec(memory_space=pltpu.VMEM)
    return pl.pallas_call(
        functools.partial(early_kernel, scale),
        out_shape=(
            jax.ShapeDtypeStruct((rows // LANES, LANES), jnp.float32),
            jax.ShapeDtypeStruct((blocks, LANES), jnp.float32),
        ),
        in_specs=[vmem] * (1 + len(parts)),
        out_specs=(vmem, vmem),
        compiler_params=pltpu.CompilerParams(vmem_limit_bytes=VMEM_LIMIT),
        name="part_statistics",
    )(a, *parts)


def home(shift):
    n = lax.axis_size("x")
    return lax.rem(lax.axis_index("x") + n - shift, n)


def last_kernel(scale, shifts, a_ref, b_ref, *refs):
    early, (row_ref, col_ref, row_part, col_part, cols) = refs[:-5], refs[-5:]
    part_statistics(scale, a_ref, [b_ref], row_part, col_part)
    row_parts = [r[...] for r in early[0::2]] + [row_part[...]]
    row_ref[...] = lse_over(jnp.stack(row_parts), 0)
    col_parts = jnp.concatenate([c[...] for c in early[1::2]] + [col_part[...]], axis=0)
    nx = len(shifts)
    blocks = b_ref.shape[0]
    for p, shift in enumerate(shifts):
        x = home(shift)
        for y in range(blocks):
            cols[pl.ds(y * nx + x, 1), :] = col_parts[p * blocks + y : p * blocks + y + 1]
    col_ref[...] = jnp.broadcast_to(cols[...][None], col_ref.shape)


def last_statistics(a, part, early, shifts, scale, copies):
    rows = a.shape[0]
    blocks = part.shape[0] * len(shifts)
    vmem = pl.BlockSpec(memory_space=pltpu.VMEM)
    flat = [leaf for pair in early for leaf in pair]
    return pl.pallas_call(
        functools.partial(last_kernel, scale, shifts),
        out_shape=(
            jax.ShapeDtypeStruct((rows // LANES, LANES), jnp.float32),
            jax.ShapeDtypeStruct((copies, blocks, LANES), jnp.float32),
        ),
        in_specs=[vmem] * (2 + len(flat)),
        out_specs=(vmem, vmem),
        scratch_shapes=[
            pltpu.VMEM((rows // LANES, LANES), jnp.float32),
            pltpu.VMEM((part.shape[0], LANES), jnp.float32),
            pltpu.VMEM((blocks, LANES), jnp.float32),
        ],
        compiler_params=pltpu.CompilerParams(vmem_limit_bytes=VMEM_LIMIT),
        name="tile_statistics",
    )(a, part, *flat)


def finish_kernel(scale, shift_up, shifts, a_ref, *refs):
    nx = len(shifts)
    b_refs = refs[:nx]
    rows_ref, cols_ref, top_ref, tot_ref, out_ref, row_lse, col_lse, held, sems = refs[nx:]
    rows = a_ref.shape[0]
    blocks, n, c = b_refs[0].shape
    width = nx * n

    lse = lse_over(rows_ref[...], 0)
    for k in range(rows // LANES):
        row_lse[pl.ds(k * LANES, LANES), :] = jnp.broadcast_to(lse[k : k + 1], (LANES, LANES)).T

    parts = cols_ref[...]
    other = top_ref[...] * LOG2E
    top = jnp.maximum(jnp.max(parts, axis=0), other)
    tot = jnp.sum(jnp.exp2(parts - top[None]), axis=0) + tot_ref[...] * jnp.exp2(other - top)
    col_lse[...] = top + jnp.log2(tot) - shift_up

    def copy(y):
        return pltpu.make_async_copy(held.at[y], out_ref.at[:, pl.ds(y * width, width)], sems.at[y])

    homes = [home(shift) for shift in shifts]
    per = WIDTH // n
    for y in range(blocks):
        for p in range(0, nx, per):
            b = jnp.concatenate([ref[y] for ref in b_refs[p : p + per]], axis=0)
            s = scores(a_ref[...], b, scale)
            for k in range(per):
                x = homes[p + k]
                part = s[:, k * n : (k + 1) * n]
                col = col_lse[pl.ds(y * nx + x, 1), :]
                e = jnp.exp2((part - row_lse[...]) + (part - col))
                held[y, :, pl.ds(pl.multiple_of(x * n, n), n)] = e.astype(held.dtype)
        copy(y).start()
    for y in range(blocks):
        copy(y).wait()


def finish(a, parts, row_parts, col_parts, col_max_other, col_sum_other, shifts, scale, shift_up):
    rows = a.shape[0]
    blocks, n, _ = parts[0].shape
    width = n * len(parts)
    vmem = pl.BlockSpec(memory_space=pltpu.VMEM)
    return pl.pallas_call(
        functools.partial(finish_kernel, scale, shift_up, shifts),
        out_shape=jax.ShapeDtypeStruct((rows, blocks * width), jnp.bfloat16),
        in_specs=[vmem] * (5 + len(parts)),
        out_specs=pl.BlockSpec(memory_space=pl.ANY),
        scratch_shapes=[
            pltpu.VMEM((rows, LANES), jnp.float32),
            pltpu.VMEM((blocks * len(parts), LANES), jnp.float32),
            pltpu.VMEM((blocks, rows, width), jnp.bfloat16),
            pltpu.SemaphoreType.DMA((blocks,)),
        ],
        compiler_params=pltpu.CompilerParams(vmem_limit_bytes=VMEM_LIMIT),
        name="confidence",
    )(a, *parts, row_parts, col_parts, col_max_other.reshape(-1, LANES), col_sum_other.reshape(-1, LANES))


def shifted(block, shift):
    n = lax.axis_size("x")
    return lax.ppermute(block, "x", [(i, (i + shift) % n) for i in range(n)])


def local(feat_a, feat_b, col_max_other, col_sum_other):
    scale = LOG2E / (feat_a.shape[1] * TEMPER)
    columns = feat_b.shape[0] * lax.axis_size(AA)
    shift_up = math.log2(float(FRAME_A) * float(columns * lax.axis_size(BA)))
    shifts = (0, 1, 3, 2)
    a = lax.all_gather(feat_a, BA, axis=0, tiled=True)
    own = spread(feat_b, "y")
    parts = [own] + [shifted(own, k) for k in shifts[1:]]
    early = [early_statistics(a, parts[:1], scale), early_statistics(a, parts[1:3], scale)]
    row_lse, col_copies = last_statistics(a, parts[3], early, shifts, scale, lax.axis_size(AA))
    row_parts = lax.all_gather(row_lse, BA, axis=0)
    col_parts = lax.all_to_all(col_copies, AA, 0, 0, tiled=True)
    return finish(a, parts, row_parts, col_parts, col_max_other, col_sum_other, shifts, scale, shift_up)


def solution(mesh):
    inner = Mesh(mesh.devices.reshape(8, 4, 8, 2), AA + BA)
    in_specs = (P(AA + BA, None), P(BA + AA, None), P(BA), P(BA))
    out_specs = P(AA, BA)
    return jax.shard_map(local, mesh=inner, in_specs=in_specs, out_specs=out_specs, check_vma=False)
```

```python
import functools
import math

import jax
import jax.numpy as jnp
from jax import lax
from jax.experimental import pallas as pl
from jax.experimental.pallas import tpu as pltpu
from jax.sharding import Mesh
from jax.sharding import PartitionSpec as P

FRAME_A = 131072
TEMPER = 0.1
LOG2E = math.log2(math.e)
AA = ("y", "x")
BA = ("z", "core")
LANES = 128
WIDTH = 256
SAFE_LOW, SAFE_HIGH = 2.0**-40, 2.0**100
VMEM_LIMIT = 48 << 20


def spread(block, axis):
    n = lax.axis_size(axis)
    return lax.all_to_all(jnp.broadcast_to(block[None], (n,) + block.shape), axis, 0, 0, tiled=True)


def scores(a, b, scale):
    return lax.dot_general(a, b, (((1,), (1,)), ((), ())), preferred_element_type=jnp.float32) * scale


def to_lanes(column):
    return jnp.sum(column.T, axis=0, keepdims=True)


def lse_over(parts, axis):
    top = jnp.max(parts, axis=axis, keepdims=True)
    return jnp.squeeze(top + jnp.log2(jnp.sum(jnp.exp2(parts - top), axis=axis, keepdims=True)), axis)


def part_statistics(scale, a_ref, b_refs, row_ref, col_ref):
    rows = a_ref.shape[0]
    blocks, n, c = b_refs[0].shape
    per = WIDTH // n
    work = [(ref, i) for ref in b_refs for i in range(0, blocks, per)]

    def put_col(t, lse):
        for k in range(per):
            col_ref[pl.ds(t * per + k, 1), :] = lse[:, k * LANES : (k + 1) * LANES]

    def put_row(lse):
        for k in range(rows // LANES):
            row_ref[pl.ds(k, 1), :] = lse[:, k * LANES : (k + 1) * LANES]

    tot = jnp.zeros((rows, LANES), jnp.float32)
    for t, (ref, i) in enumerate(work):
        e = jnp.exp2(scores(a_ref[...], ref[i : i + per].reshape(WIDTH, c), scale))
        put_col(t, jnp.log2(jnp.sum(e, axis=0, keepdims=True)))
        for k in range(per):
            tot = tot + e[:, k * LANES : (k + 1) * LANES]
    row_tot = to_lanes(tot)
    put_row(jnp.log2(row_tot))
    in_range = (jnp.min(row_tot) > SAFE_LOW) & (jnp.max(row_tot) < SAFE_HIGH)

    @pl.when(jnp.logical_not(in_range))
    def _():
        top = jnp.full((rows, 1), -jnp.inf, jnp.float32)
        for t, (ref, i) in enumerate(work):
            s = scores(a_ref[...], ref[i : i + per].reshape(WIDTH, c), scale)
            col_top = jnp.max(s, axis=0, keepdims=True)
            put_col(t, col_top + jnp.log2(jnp.sum(jnp.exp2(s - col_top), axis=0, keepdims=True)))
            top = jnp.maximum(top, jnp.max(s, axis=1, keepdims=True))
        tot = jnp.zeros((rows, LANES), jnp.float32)
        for ref, i in work:
            e = jnp.exp2(scores(a_ref[...], ref[i : i + per].reshape(WIDTH, c), scale) - top)
            for k in range(per):
                tot = tot + e[:, k * LANES : (k + 1) * LANES]
        row_top = jnp.broadcast_to(top, (rows, LANES)).T[:1]
        put_row(row_top + jnp.log2(to_lanes(tot)))


def early_kernel(scale, a_ref, *refs):
    part_statistics(scale, a_ref, refs[:-2], *refs[-2:])


def early_statistics(a, parts, scale):
    rows = a.shape[0]
    blocks = sum(p.shape[0] for p in parts)
    vmem = pl.BlockSpec(memory_space=pltpu.VMEM)
    return pl.pallas_call(
        functools.partial(early_kernel, scale),
        out_shape=(
            jax.ShapeDtypeStruct((rows // LANES, LANES), jnp.float32),
            jax.ShapeDtypeStruct((blocks, LANES), jnp.float32),
        ),
        in_specs=[vmem] * (1 + len(parts)),
        out_specs=(vmem, vmem),
        compiler_params=pltpu.CompilerParams(vmem_limit_bytes=VMEM_LIMIT),
        name="part_statistics",
    )(a, *parts)


def home(shift):
    n = lax.axis_size("x")
    return lax.rem(lax.axis_index("x") + n - shift, n)


def last_kernel(scale, shifts, count, a_ref, *refs):
    b_refs, early, (row_ref, col_ref, row_part, col_part, cols) = refs[:count], refs[count:-5], refs[-5:]
    part_statistics(scale, a_ref, b_refs, row_part, col_part)
    row_parts = [r[...] for r in early[0::2]] + [row_part[...]]
    row_ref[...] = lse_over(jnp.stack(row_parts), 0)
    col_parts = jnp.concatenate([c[...] for c in early[1::2]] + [col_part[...]], axis=0)
    nx = len(shifts)
    blocks = b_refs[0].shape[0]
    for p, shift in enumerate(shifts):
        x = home(shift)
        for y in range(blocks):
            cols[pl.ds(y * nx + x, 1), :] = col_parts[p * blocks + y : p * blocks + y + 1]
    col_ref[...] = jnp.broadcast_to(cols[...][None], col_ref.shape)


def last_statistics(a, parts, early, shifts, scale, copies):
    rows = a.shape[0]
    last = parts[0].shape[0] * len(parts)
    blocks = parts[0].shape[0] * len(shifts)
    vmem = pl.BlockSpec(memory_space=pltpu.VMEM)
    flat = [leaf for pair in early for leaf in pair]
    return pl.pallas_call(
        functools.partial(last_kernel, scale, shifts, len(parts)),
        out_shape=(
            jax.ShapeDtypeStruct((rows // LANES, LANES), jnp.float32),
            jax.ShapeDtypeStruct((copies, blocks, LANES), jnp.float32),
        ),
        in_specs=[vmem] * (1 + len(parts) + len(flat)),
        out_specs=(vmem, vmem),
        scratch_shapes=[
            pltpu.VMEM((rows // LANES, LANES), jnp.float32),
            pltpu.VMEM((last, LANES), jnp.float32),
            pltpu.VMEM((blocks, LANES), jnp.float32),
        ],
        compiler_params=pltpu.CompilerParams(vmem_limit_bytes=VMEM_LIMIT),
        name="tile_statistics",
    )(a, *parts, *flat)


def finish_kernel(scale, shift_up, shifts, a_ref, *refs):
    nx = len(shifts)
    b_refs = refs[:nx]
    rows_ref, cols_ref, top_ref, tot_ref, out_ref, row_lse, col_lse, held, sems = refs[nx:]
    rows = a_ref.shape[0]
    blocks, n, c = b_refs[0].shape
    width = nx * n

    lse = lse_over(rows_ref[...], 0)
    for k in range(rows // LANES):
        row_lse[pl.ds(k * LANES, LANES), :] = jnp.broadcast_to(lse[k : k + 1], (LANES, LANES)).T

    parts = cols_ref[...]
    other = top_ref[...] * LOG2E
    top = jnp.maximum(jnp.max(parts, axis=0), other)
    tot = jnp.sum(jnp.exp2(parts - top[None]), axis=0) + tot_ref[...] * jnp.exp2(other - top)
    col_lse[...] = top + jnp.log2(tot) - shift_up

    def copy(y):
        return pltpu.make_async_copy(held.at[y], out_ref.at[:, pl.ds(y * width, width)], sems.at[y])

    homes = [home(shift) for shift in shifts]
    per = WIDTH // n
    for y in range(blocks):
        for p in range(0, nx, per):
            b = jnp.concatenate([ref[y] for ref in b_refs[p : p + per]], axis=0)
            s = scores(a_ref[...], b, scale)
            for k in range(per):
                x = homes[p + k]
                part = s[:, k * n : (k + 1) * n]
                col = col_lse[pl.ds(y * nx + x, 1), :]
                e = jnp.exp2((part - row_lse[...]) + (part - col))
                held[y, :, pl.ds(pl.multiple_of(x * n, n), n)] = e.astype(held.dtype)
        copy(y).start()
    for y in range(blocks):
        copy(y).wait()


def finish(a, parts, row_parts, col_parts, col_max_other, col_sum_other, shifts, scale, shift_up):
    rows = a.shape[0]
    blocks, n, _ = parts[0].shape
    width = n * len(parts)
    vmem = pl.BlockSpec(memory_space=pltpu.VMEM)
    return pl.pallas_call(
        functools.partial(finish_kernel, scale, shift_up, shifts),
        out_shape=jax.ShapeDtypeStruct((rows, blocks * width), jnp.bfloat16),
        in_specs=[vmem] * (5 + len(parts)),
        out_specs=pl.BlockSpec(memory_space=pl.ANY),
        scratch_shapes=[
            pltpu.VMEM((rows, LANES), jnp.float32),
            pltpu.VMEM((blocks * len(parts), LANES), jnp.float32),
            pltpu.VMEM((blocks, rows, width), jnp.bfloat16),
            pltpu.SemaphoreType.DMA((blocks,)),
        ],
        compiler_params=pltpu.CompilerParams(vmem_limit_bytes=VMEM_LIMIT),
        name="confidence",
    )(a, *parts, row_parts, col_parts, col_max_other.reshape(-1, LANES), col_sum_other.reshape(-1, LANES))


def shifted(block, shift):
    n = lax.axis_size("x")
    return lax.ppermute(block, "x", [(i, (i + shift) % n) for i in range(n)])


def local(feat_a, feat_b, col_max_other, col_sum_other):
    scale = LOG2E / (feat_a.shape[1] * TEMPER)
    columns = feat_b.shape[0] * lax.axis_size(AA)
    shift_up = math.log2(float(FRAME_A) * float(columns * lax.axis_size(BA)))
    shifts = (0, 2, 1, 3)
    own = spread(feat_b, "y")
    feat_a, own = lax.optimization_barrier((feat_a, own))
    a = spread(feat_a, BA).reshape(-1, feat_a.shape[1])
    parts = [own] + [shifted(own, k) for k in shifts[1:]]
    early = [early_statistics(a, parts[:1], scale), early_statistics(a, parts[1:2], scale)]
    row_lse, col_copies = last_statistics(a, parts[2:], early, shifts, scale, lax.axis_size(AA))
    row_parts = lax.all_gather(row_lse, BA, axis=0)
    col_parts = lax.all_to_all(col_copies, AA, 0, 0, tiled=True)
    return finish(a, parts, row_parts, col_parts, col_max_other, col_sum_other, shifts, scale, shift_up)


def solution(mesh):
    inner = Mesh(mesh.devices.reshape(8, 4, 8, 2), AA + BA)
    in_specs = (P(AA + BA, None), P(BA + AA, None), P(BA), P(BA))
    out_specs = P(AA, BA)
    return jax.shard_map(local, mesh=inner, in_specs=in_specs, out_specs=out_specs, check_vma=False)
```

```python
import functools
import math

import jax
import jax.numpy as jnp
from jax import lax
from jax.experimental import pallas as pl
from jax.experimental.pallas import tpu as pltpu
from jax.sharding import Mesh
from jax.sharding import PartitionSpec as P

FRAME_A = 131072
TEMPER = 0.1
LOG2E = math.log2(math.e)
AA = ("y", "x")
BA = ("z", "core")
LANES = 128
WIDTH = 256
SAFE_LOW, SAFE_HIGH = 2.0**-40, 2.0**100
VMEM_LIMIT = 48 << 20


def spread(block, axis):
    n = lax.axis_size(axis)
    return lax.all_to_all(jnp.broadcast_to(block[None], (n,) + block.shape), axis, 0, 0, tiled=True)


def scores(a, b, scale):
    return lax.dot_general(a, b, (((1,), (1,)), ((), ())), preferred_element_type=jnp.float32) * scale


def to_lanes(column):
    return jnp.sum(column.T, axis=0, keepdims=True)


def lse_over(parts, axis):
    top = jnp.max(parts, axis=axis, keepdims=True)
    return jnp.squeeze(top + jnp.log2(jnp.sum(jnp.exp2(parts - top), axis=axis, keepdims=True)), axis)


def part_statistics(scale, a_ref, b_refs, row_ref, col_ref):
    rows = a_ref.shape[0]
    blocks, n, c = b_refs[0].shape
    per = WIDTH // n
    work = [(ref, i) for ref in b_refs for i in range(0, blocks, per)]

    def put_col(t, lse):
        for k in range(per):
            col_ref[pl.ds(t * per + k, 1), :] = lse[:, k * LANES : (k + 1) * LANES]

    def put_row(lse):
        for k in range(rows // LANES):
            row_ref[pl.ds(k, 1), :] = lse[:, k * LANES : (k + 1) * LANES]

    tot = jnp.zeros((rows, LANES), jnp.float32)
    for t, (ref, i) in enumerate(work):
        e = jnp.exp2(scores(a_ref[...], ref[i : i + per].reshape(WIDTH, c), scale))
        put_col(t, jnp.log2(jnp.sum(e, axis=0, keepdims=True)))
        for k in range(per):
            tot = tot + e[:, k * LANES : (k + 1) * LANES]
    row_tot = to_lanes(tot)
    put_row(jnp.log2(row_tot))
    in_range = (jnp.min(row_tot) > SAFE_LOW) & (jnp.max(row_tot) < SAFE_HIGH)

    @pl.when(jnp.logical_not(in_range))
    def _():
        top = jnp.full((rows, 1), -jnp.inf, jnp.float32)
        tot = jnp.zeros((rows, LANES), jnp.float32)
        for q, ref in enumerate(b_refs):

            def first(i, top, q=q, ref=ref):
                s = scores(a_ref[...], ref[pl.ds(i * per, per)].reshape(WIDTH, c), scale)
                col_top = jnp.max(s, axis=0, keepdims=True)
                put_col(q * (blocks // per) + i, col_top + jnp.log2(jnp.sum(jnp.exp2(s - col_top), axis=0, keepdims=True)))
                return jnp.maximum(top, jnp.max(s, axis=1, keepdims=True))

            top = lax.fori_loop(0, blocks // per, first, top)
        for ref in b_refs:

            def second(i, tot, ref=ref):
                e = jnp.exp2(scores(a_ref[...], ref[pl.ds(i * per, per)].reshape(WIDTH, c), scale) - top)
                for k in range(per):
                    tot = tot + e[:, k * LANES : (k + 1) * LANES]
                return tot

            tot = lax.fori_loop(0, blocks // per, second, tot)
        row_top = jnp.broadcast_to(top, (rows, LANES)).T[:1]
        put_row(row_top + jnp.log2(to_lanes(tot)))


def early_kernel(scale, a_ref, *refs):
    part_statistics(scale, a_ref, refs[:-2], *refs[-2:])


def early_statistics(a, parts, scale):
    rows = a.shape[0]
    blocks = sum(p.shape[0] for p in parts)
    vmem = pl.BlockSpec(memory_space=pltpu.VMEM)
    return pl.pallas_call(
        functools.partial(early_kernel, scale),
        out_shape=(
            jax.ShapeDtypeStruct((rows // LANES, LANES), jnp.float32),
            jax.ShapeDtypeStruct((blocks, LANES), jnp.float32),
        ),
        in_specs=[vmem] * (1 + len(parts)),
        out_specs=(vmem, vmem),
        compiler_params=pltpu.CompilerParams(vmem_limit_bytes=VMEM_LIMIT),
        name="part_statistics",
    )(a, *parts)


def home(shift):
    n = lax.axis_size("x")
    return lax.rem(lax.axis_index("x") + n - shift, n)


def last_kernel(scale, shifts, count, a_ref, *refs):
    b_refs, early, (row_ref, col_ref, row_part, col_part, cols) = refs[:count], refs[count:-5], refs[-5:]
    part_statistics(scale, a_ref, b_refs, row_part, col_part)
    row_parts = [r[...] for r in early[0::2]] + [row_part[...]]
    row_ref[...] = lse_over(jnp.stack(row_parts), 0)
    col_parts = jnp.concatenate([c[...] for c in early[1::2]] + [col_part[...]], axis=0)
    nx = len(shifts)
    blocks = b_refs[0].shape[0]
    for p, shift in enumerate(shifts):
        x = home(shift)
        for y in range(blocks):
            cols[pl.ds(y * nx + x, 1), :] = col_parts[p * blocks + y : p * blocks + y + 1]
    col_ref[...] = jnp.broadcast_to(cols[...][None], col_ref.shape)


def last_statistics(a, parts, early, shifts, scale, copies):
    rows = a.shape[0]
    last = parts[0].shape[0] * len(parts)
    blocks = parts[0].shape[0] * len(shifts)
    vmem = pl.BlockSpec(memory_space=pltpu.VMEM)
    flat = [leaf for pair in early for leaf in pair]
    return pl.pallas_call(
        functools.partial(last_kernel, scale, shifts, len(parts)),
        out_shape=(
            jax.ShapeDtypeStruct((rows // LANES, LANES), jnp.float32),
            jax.ShapeDtypeStruct((copies, blocks, LANES), jnp.float32),
        ),
        in_specs=[vmem] * (1 + len(parts) + len(flat)),
        out_specs=(vmem, vmem),
        scratch_shapes=[
            pltpu.VMEM((rows // LANES, LANES), jnp.float32),
            pltpu.VMEM((last, LANES), jnp.float32),
            pltpu.VMEM((blocks, LANES), jnp.float32),
        ],
        compiler_params=pltpu.CompilerParams(vmem_limit_bytes=VMEM_LIMIT),
        name="tile_statistics",
    )(a, *parts, *flat)


def finish_kernel(scale, shift_up, shifts, a_ref, *refs):
    nx = len(shifts)
    b_refs = refs[:nx]
    rows_ref, cols_ref, top_ref, tot_ref, out_ref, row_lse, col_lse, held, sems = refs[nx:]
    rows = a_ref.shape[0]
    blocks, n, c = b_refs[0].shape
    width = nx * n

    lse = lse_over(rows_ref[...], 0)
    for k in range(rows // LANES):
        row_lse[pl.ds(k * LANES, LANES), :] = jnp.broadcast_to(lse[k : k + 1], (LANES, LANES)).T

    parts = cols_ref[...]
    other = top_ref[...] * LOG2E
    top = jnp.maximum(jnp.max(parts, axis=0), other)
    tot = jnp.sum(jnp.exp2(parts - top[None]), axis=0) + tot_ref[...] * jnp.exp2(other - top)
    col_lse[...] = top + jnp.log2(tot) - shift_up

    def copy(y):
        return pltpu.make_async_copy(held.at[y], out_ref.at[:, pl.ds(y * width, width)], sems.at[y])

    homes = [home(shift) for shift in shifts]
    per = WIDTH // n
    for y in range(blocks):
        for p in range(0, nx, per):
            b = jnp.concatenate([ref[y] for ref in b_refs[p : p + per]], axis=0)
            s = scores(a_ref[...], b, scale)
            for k in range(per):
                x = homes[p + k]
                part = s[:, k * n : (k + 1) * n]
                col = col_lse[pl.ds(y * nx + x, 1), :]
                e = jnp.exp2((part - row_lse[...]) + (part - col))
                held[y, :, pl.ds(pl.multiple_of(x * n, n), n)] = e.astype(held.dtype)
        copy(y).start()
    for y in range(blocks):
        copy(y).wait()


def finish(a, parts, row_parts, col_parts, col_max_other, col_sum_other, shifts, scale, shift_up):
    rows = a.shape[0]
    blocks, n, _ = parts[0].shape
    width = n * len(parts)
    vmem = pl.BlockSpec(memory_space=pltpu.VMEM)
    return pl.pallas_call(
        functools.partial(finish_kernel, scale, shift_up, shifts),
        out_shape=jax.ShapeDtypeStruct((rows, blocks * width), jnp.bfloat16),
        in_specs=[vmem] * (5 + len(parts)),
        out_specs=pl.BlockSpec(memory_space=pl.ANY),
        scratch_shapes=[
            pltpu.VMEM((rows, LANES), jnp.float32),
            pltpu.VMEM((blocks * len(parts), LANES), jnp.float32),
            pltpu.VMEM((blocks, rows, width), jnp.bfloat16),
            pltpu.SemaphoreType.DMA((blocks,)),
        ],
        compiler_params=pltpu.CompilerParams(vmem_limit_bytes=VMEM_LIMIT),
        name="confidence",
    )(a, *parts, row_parts, col_parts, col_max_other.reshape(-1, LANES), col_sum_other.reshape(-1, LANES))


def shifted(block, shift):
    n = lax.axis_size("x")
    return lax.ppermute(block, "x", [(i, (i + shift) % n) for i in range(n)])


def local(feat_a, feat_b, col_max_other, col_sum_other):
    scale = LOG2E / (feat_a.shape[1] * TEMPER)
    columns = feat_b.shape[0] * lax.axis_size(AA)
    shift_up = math.log2(float(FRAME_A) * float(columns * lax.axis_size(BA)))
    shifts = (0, 2, 1, 3)
    own = spread(feat_b, "y")
    feat_a, own = lax.optimization_barrier((feat_a, own))
    a = spread(feat_a, BA).reshape(-1, feat_a.shape[1])
    parts = [own] + [shifted(own, k) for k in shifts[1:]]
    early = [early_statistics(a, parts[:2], scale)]
    row_lse, col_copies = last_statistics(a, parts[2:], early, shifts, scale, lax.axis_size(AA))
    row_parts = lax.all_gather(row_lse, BA, axis=0)
    col_parts = lax.all_to_all(col_copies, AA[::-1], 0, 0, tiled=True)
    return finish(a, parts, row_parts, col_parts, col_max_other, col_sum_other, shifts, scale, shift_up)


def solution(mesh):
    inner = Mesh(mesh.devices.reshape(8, 4, 8, 2), AA + BA)
    in_specs = (P(AA + BA, None), P(BA + AA, None), P(BA), P(BA))
    out_specs = P(AA, BA)
    return jax.shard_map(local, mesh=inner, in_specs=in_specs, out_specs=out_specs, check_vma=False)
```

```python
import functools
import math

import jax
import jax.numpy as jnp
from jax import lax
from jax.experimental import pallas as pl
from jax.experimental.pallas import tpu as pltpu
from jax.sharding import Mesh
from jax.sharding import PartitionSpec as P

FRAME_A = 131072
TEMPER = 0.1
LOG2E = math.log2(math.e)
AA = ("y", "x")
BA = ("z", "core")
LANES = 128
Y_ORDER = (3, 4, 2, 5, 1, 6, 0, 7)
WIDTH = 256
SAFE_LOW, SAFE_HIGH = 2.0**-40, 2.0**100
VMEM_LIMIT = 48 << 20


def spread(block, axis, order=None):
    n = lax.axis_size(axis)
    copies = jnp.broadcast_to(block[None], (n,) + block.shape)
    return lax.all_to_all(copies, axis, 0, 0, tiled=True, axis_index_groups=None if order is None else [list(order)])


def scores(a, b, scale):
    return lax.dot_general(a, b, (((1,), (1,)), ((), ())), preferred_element_type=jnp.float32) * scale


def to_lanes(column):
    return jnp.sum(column.T, axis=0, keepdims=True)


def lse_over(parts, axis):
    top = jnp.max(parts, axis=axis, keepdims=True)
    return jnp.squeeze(top + jnp.log2(jnp.sum(jnp.exp2(parts - top), axis=axis, keepdims=True)), axis)


def part_statistics(scale, a_ref, b_refs, row_ref, col_ref):
    rows = a_ref.shape[0]
    blocks, n, c = b_refs[0].shape
    per = WIDTH // n
    work = [(ref, i) for ref in b_refs for i in range(0, blocks, per)]

    def put_col(t, lse):
        for k in range(per):
            col_ref[pl.ds(t * per + k, 1), :] = lse[:, k * LANES : (k + 1) * LANES]

    def put_row(lse):
        for k in range(rows // LANES):
            row_ref[pl.ds(k, 1), :] = lse[:, k * LANES : (k + 1) * LANES]

    tot = jnp.zeros((rows, LANES), jnp.float32)
    for t, (ref, i) in enumerate(work):
        e = jnp.exp2(scores(a_ref[...], ref[i : i + per].reshape(WIDTH, c), scale))
        put_col(t, jnp.log2(jnp.sum(e, axis=0, keepdims=True)))
        for k in range(per):
            tot = tot + e[:, k * LANES : (k + 1) * LANES]
    row_tot = to_lanes(tot)
    put_row(jnp.log2(row_tot))
    in_range = (jnp.min(row_tot) > SAFE_LOW) & (jnp.max(row_tot) < SAFE_HIGH)

    @pl.when(jnp.logical_not(in_range))
    def _():
        top = jnp.full((rows, 1), -jnp.inf, jnp.float32)
        tot = jnp.zeros((rows, LANES), jnp.float32)
        for q, ref in enumerate(b_refs):

            def first(i, top, q=q, ref=ref):
                s = scores(a_ref[...], ref[pl.ds(i * per, per)].reshape(WIDTH, c), scale)
                col_top = jnp.max(s, axis=0, keepdims=True)
                put_col(q * (blocks // per) + i, col_top + jnp.log2(jnp.sum(jnp.exp2(s - col_top), axis=0, keepdims=True)))
                return jnp.maximum(top, jnp.max(s, axis=1, keepdims=True))

            top = lax.fori_loop(0, blocks // per, first, top)
        for ref in b_refs:

            def second(i, tot, ref=ref):
                e = jnp.exp2(scores(a_ref[...], ref[pl.ds(i * per, per)].reshape(WIDTH, c), scale) - top)
                for k in range(per):
                    tot = tot + e[:, k * LANES : (k + 1) * LANES]
                return tot

            tot = lax.fori_loop(0, blocks // per, second, tot)
        row_top = jnp.broadcast_to(top, (rows, LANES)).T[:1]
        put_row(row_top + jnp.log2(to_lanes(tot)))


def early_kernel(scale, a_ref, *refs):
    part_statistics(scale, a_ref, refs[:-2], *refs[-2:])


def early_statistics(a, parts, scale):
    rows = a.shape[0]
    blocks = sum(p.shape[0] for p in parts)
    vmem = pl.BlockSpec(memory_space=pltpu.VMEM)
    return pl.pallas_call(
        functools.partial(early_kernel, scale),
        out_shape=(
            jax.ShapeDtypeStruct((rows // LANES, LANES), jnp.float32),
            jax.ShapeDtypeStruct((blocks, LANES), jnp.float32),
        ),
        in_specs=[vmem] * (1 + len(parts)),
        out_specs=(vmem, vmem),
        compiler_params=pltpu.CompilerParams(vmem_limit_bytes=VMEM_LIMIT),
        name="part_statistics",
    )(a, *parts)


def home(shift):
    n = lax.axis_size("x")
    return lax.rem(lax.axis_index("x") + n - shift, n)


def last_kernel(scale, shifts, count, a_ref, *refs):
    b_refs, early, (row_ref, col_ref, row_part, col_part, cols) = refs[:count], refs[count:-5], refs[-5:]
    part_statistics(scale, a_ref, b_refs, row_part, col_part)
    row_parts = [r[...] for r in early[0::2]] + [row_part[...]]
    row_ref[...] = lse_over(jnp.stack(row_parts), 0)
    col_parts = jnp.concatenate([c[...] for c in early[1::2]] + [col_part[...]], axis=0)
    nx = len(shifts)
    blocks = b_refs[0].shape[0]
    for p, shift in enumerate(shifts):
        x = home(shift)
        for i, y in enumerate(Y_ORDER):
            cols[pl.ds(y * nx + x, 1), :] = col_parts[p * blocks + i : p * blocks + i + 1]
    col_ref[...] = jnp.broadcast_to(cols[...][None], col_ref.shape)


def last_statistics(a, parts, early, shifts, scale, copies):
    rows = a.shape[0]
    last = parts[0].shape[0] * len(parts)
    blocks = parts[0].shape[0] * len(shifts)
    vmem = pl.BlockSpec(memory_space=pltpu.VMEM)
    flat = [leaf for pair in early for leaf in pair]
    return pl.pallas_call(
        functools.partial(last_kernel, scale, shifts, len(parts)),
        out_shape=(
            jax.ShapeDtypeStruct((rows // LANES, LANES), jnp.float32),
            jax.ShapeDtypeStruct((copies, blocks, LANES), jnp.float32),
        ),
        in_specs=[vmem] * (1 + len(parts) + len(flat)),
        out_specs=(vmem, vmem),
        scratch_shapes=[
            pltpu.VMEM((rows // LANES, LANES), jnp.float32),
            pltpu.VMEM((last, LANES), jnp.float32),
            pltpu.VMEM((blocks, LANES), jnp.float32),
        ],
        compiler_params=pltpu.CompilerParams(vmem_limit_bytes=VMEM_LIMIT),
        name="tile_statistics",
    )(a, *parts, *flat)


def finish_kernel(scale, shift_up, shifts, a_ref, *refs):
    nx = len(shifts)
    b_refs = refs[:nx]
    rows_ref, cols_ref, top_ref, tot_ref, out_ref, row_lse, col_lse, held, sems = refs[nx:]
    rows = a_ref.shape[0]
    blocks, n, c = b_refs[0].shape
    width = nx * n

    lse = lse_over(rows_ref[...], 0)
    for k in range(rows // LANES):
        row_lse[pl.ds(k * LANES, LANES), :] = jnp.broadcast_to(lse[k : k + 1], (LANES, LANES)).T

    parts = cols_ref[...]
    other = top_ref[...] * LOG2E
    top = jnp.maximum(jnp.max(parts, axis=0), other)
    tot = jnp.sum(jnp.exp2(parts - top[None]), axis=0) + tot_ref[...] * jnp.exp2(other - top)
    col_lse[...] = top + jnp.log2(tot) - shift_up

    def copy(y):
        return pltpu.make_async_copy(held.at[y], out_ref.at[:, pl.ds(y * width, width)], sems.at[y])

    homes = [home(shift) for shift in shifts]
    per = WIDTH // n
    for i, y in enumerate(Y_ORDER):
        for p in range(0, nx, per):
            b = jnp.concatenate([ref[i] for ref in b_refs[p : p + per]], axis=0)
            s = scores(a_ref[...], b, scale)
            for k in range(per):
                x = homes[p + k]
                part = s[:, k * n : (k + 1) * n]
                col = col_lse[pl.ds(y * nx + x, 1), :]
                e = jnp.exp2((part - row_lse[...]) + (part - col))
                held[y, :, pl.ds(pl.multiple_of(x * n, n), n)] = e.astype(held.dtype)
        copy(y).start()
    for y in range(blocks):
        copy(y).wait()


def finish(a, parts, row_parts, col_parts, col_max_other, col_sum_other, shifts, scale, shift_up):
    rows = a.shape[0]
    blocks, n, _ = parts[0].shape
    width = n * len(parts)
    vmem = pl.BlockSpec(memory_space=pltpu.VMEM)
    return pl.pallas_call(
        functools.partial(finish_kernel, scale, shift_up, shifts),
        out_shape=jax.ShapeDtypeStruct((rows, blocks * width), jnp.bfloat16),
        in_specs=[vmem] * (5 + len(parts)),
        out_specs=pl.BlockSpec(memory_space=pl.ANY),
        scratch_shapes=[
            pltpu.VMEM((rows, LANES), jnp.float32),
            pltpu.VMEM((blocks * len(parts), LANES), jnp.float32),
            pltpu.VMEM((blocks, rows, width), jnp.bfloat16),
            pltpu.SemaphoreType.DMA((blocks,)),
        ],
        compiler_params=pltpu.CompilerParams(vmem_limit_bytes=VMEM_LIMIT),
        name="confidence",
    )(a, *parts, row_parts, col_parts, col_max_other.reshape(-1, LANES), col_sum_other.reshape(-1, LANES))


def shifted(block, shift):
    n = lax.axis_size("x")
    return lax.ppermute(block, "x", [(i, (i + shift) % n) for i in range(n)])


def local(feat_a, feat_b, col_max_other, col_sum_other):
    scale = LOG2E / (feat_a.shape[1] * TEMPER)
    columns = feat_b.shape[0] * lax.axis_size(AA)
    shift_up = math.log2(float(FRAME_A) * float(columns * lax.axis_size(BA)))
    shifts = (0, 2, 1, 3)
    own = spread(feat_b, "y", Y_ORDER)
    feat_a, own = lax.optimization_barrier((feat_a, own))
    a = spread(feat_a, BA).reshape(-1, feat_a.shape[1])
    parts = [own] + [shifted(own, k) for k in shifts[1:]]
    early = [early_statistics(a, parts[:2], scale)]
    row_lse, col_copies = last_statistics(a, parts[2:], early, shifts, scale, lax.axis_size(AA))
    row_parts = lax.all_gather(row_lse, BA, axis=0)
    col_parts = lax.all_to_all(col_copies, AA[::-1], 0, 0, tiled=True)
    return finish(a, parts, row_parts, col_parts, col_max_other, col_sum_other, shifts, scale, shift_up)


def solution(mesh):
    inner = Mesh(mesh.devices.reshape(8, 4, 8, 2), AA + BA)
    in_specs = (P(AA + BA, None), P(BA + AA, None), P(BA), P(BA))
    out_specs = P(AA, BA)
    return jax.shard_map(local, mesh=inner, in_specs=in_specs, out_specs=out_specs, check_vma=False)
```

```python
import functools
import math

import jax
import jax.numpy as jnp
from jax import lax
from jax.experimental import pallas as pl
from jax.experimental.pallas import tpu as pltpu
from jax.sharding import Mesh
from jax.sharding import PartitionSpec as P

FRAME_A = 131072
TEMPER = 0.1
LOG2E = math.log2(math.e)
AA = ("y", "x")
BA = ("z", "core")
LANES = 128
Y_ORDER = (3, 4, 2, 5, 1, 6, 0, 7)
WIDTH = 256
SAFE_LOW, SAFE_HIGH = 2.0**-40, 2.0**100
VMEM_LIMIT = 48 << 20


def spread(block, axis, order=None):
    n = lax.axis_size(axis)
    copies = jnp.broadcast_to(block[None], (n,) + block.shape)
    return lax.all_to_all(copies, axis, 0, 0, tiled=True, axis_index_groups=None if order is None else [list(order)])


def scores(a, b, scale):
    return lax.dot_general(a, b, (((1,), (1,)), ((), ())), preferred_element_type=jnp.float32) * scale


def to_lanes(column):
    return jnp.sum(column.T, axis=0, keepdims=True)


def lse_over(parts, axis):
    top = jnp.max(parts, axis=axis, keepdims=True)
    return jnp.squeeze(top + jnp.log2(jnp.sum(jnp.exp2(parts - top), axis=axis, keepdims=True)), axis)


def part_statistics(scale, a_ref, b_refs, row_ref, col_ref):
    rows = a_ref.shape[0]
    blocks, n, c = b_refs[0].shape
    per = WIDTH // n
    work = [(ref, i) for ref in b_refs for i in range(0, blocks, per)]

    def put_col(t, lse):
        for k in range(per):
            col_ref[pl.ds(t * per + k, 1), :] = lse[:, k * LANES : (k + 1) * LANES]

    def put_row(lse):
        for k in range(rows // LANES):
            row_ref[pl.ds(k, 1), :] = lse[:, k * LANES : (k + 1) * LANES]

    tot = jnp.zeros((rows, LANES), jnp.float32)
    for t, (ref, i) in enumerate(work):
        e = jnp.exp2(scores(a_ref[...], ref[i : i + per].reshape(WIDTH, c), scale))
        put_col(t, jnp.log2(jnp.sum(e, axis=0, keepdims=True)))
        for k in range(per):
            tot = tot + e[:, k * LANES : (k + 1) * LANES]
    row_tot = to_lanes(tot)
    put_row(jnp.log2(row_tot))
    in_range = (jnp.min(row_tot) > SAFE_LOW) & (jnp.max(row_tot) < SAFE_HIGH)

    @pl.when(jnp.logical_not(in_range))
    def _():
        top = jnp.full((rows, 1), -jnp.inf, jnp.float32)
        tot = jnp.zeros((rows, LANES), jnp.float32)
        for q, ref in enumerate(b_refs):

            def first(i, top, q=q, ref=ref):
                s = scores(a_ref[...], ref[pl.ds(i * per, per)].reshape(WIDTH, c), scale)
                col_top = jnp.max(s, axis=0, keepdims=True)
                put_col(q * (blocks // per) + i, col_top + jnp.log2(jnp.sum(jnp.exp2(s - col_top), axis=0, keepdims=True)))
                return jnp.maximum(top, jnp.max(s, axis=1, keepdims=True))

            top = lax.fori_loop(0, blocks // per, first, top)
        for ref in b_refs:

            def second(i, tot, ref=ref):
                e = jnp.exp2(scores(a_ref[...], ref[pl.ds(i * per, per)].reshape(WIDTH, c), scale) - top)
                for k in range(per):
                    tot = tot + e[:, k * LANES : (k + 1) * LANES]
                return tot

            tot = lax.fori_loop(0, blocks // per, second, tot)
        row_top = jnp.broadcast_to(top, (rows, LANES)).T[:1]
        put_row(row_top + jnp.log2(to_lanes(tot)))


def early_kernel(scale, a_ref, *refs):
    part_statistics(scale, a_ref, refs[:-2], *refs[-2:])


def early_statistics(a, parts, scale):
    rows = a.shape[0]
    blocks = sum(p.shape[0] for p in parts)
    vmem = pl.BlockSpec(memory_space=pltpu.VMEM)
    return pl.pallas_call(
        functools.partial(early_kernel, scale),
        out_shape=(
            jax.ShapeDtypeStruct((rows // LANES, LANES), jnp.float32),
            jax.ShapeDtypeStruct((blocks, LANES), jnp.float32),
        ),
        in_specs=[vmem] * (1 + len(parts)),
        out_specs=(vmem, vmem),
        compiler_params=pltpu.CompilerParams(vmem_limit_bytes=VMEM_LIMIT),
        name="part_statistics",
    )(a, *parts)


def home(shift):
    n = lax.axis_size("x")
    return lax.rem(lax.axis_index("x") + n - shift, n)


def last_kernel(scale, shifts, count, a_ref, *refs):
    b_refs, early, (row_ref, col_ref, row_part, col_part, cols) = refs[:count], refs[count:-5], refs[-5:]
    part_statistics(scale, a_ref, b_refs, row_part, col_part)
    row_parts = [r[...] for r in early[0::2]] + [row_part[...]]
    row_ref[...] = lse_over(jnp.stack(row_parts), 0)
    col_parts = jnp.concatenate([c[...] for c in early[1::2]] + [col_part[...]], axis=0)
    nx = len(shifts)
    blocks = b_refs[0].shape[0]
    for p, shift in enumerate(shifts):
        x = home(shift)
        for i, y in enumerate(Y_ORDER):
            cols[pl.ds(y * nx + x, 1), :] = col_parts[p * blocks + i : p * blocks + i + 1]
    col_ref[...] = jnp.broadcast_to(cols[...][None], col_ref.shape)


def last_statistics(a, parts, early, shifts, scale, copies):
    rows = a.shape[0]
    last = parts[0].shape[0] * len(parts)
    blocks = parts[0].shape[0] * len(shifts)
    vmem = pl.BlockSpec(memory_space=pltpu.VMEM)
    flat = [leaf for pair in early for leaf in pair]
    return pl.pallas_call(
        functools.partial(last_kernel, scale, shifts, len(parts)),
        out_shape=(
            jax.ShapeDtypeStruct((rows // LANES, LANES), jnp.float32),
            jax.ShapeDtypeStruct((copies, blocks, LANES), jnp.float32),
        ),
        in_specs=[vmem] * (1 + len(parts) + len(flat)),
        out_specs=(vmem, vmem),
        scratch_shapes=[
            pltpu.VMEM((rows // LANES, LANES), jnp.float32),
            pltpu.VMEM((last, LANES), jnp.float32),
            pltpu.VMEM((blocks, LANES), jnp.float32),
        ],
        compiler_params=pltpu.CompilerParams(vmem_limit_bytes=VMEM_LIMIT),
        name="tile_statistics",
    )(a, *parts, *flat)


def finish_kernel(scale, shift_up, shifts, a_ref, *refs):
    nx = len(shifts)
    b_refs = refs[:nx]
    rows_ref, cols_ref, top_ref, tot_ref, out_ref, row_lse, col_lse, held, sems = refs[nx:]
    rows = a_ref.shape[0]
    blocks, n, c = b_refs[0].shape
    width = nx * n

    lse = lse_over(rows_ref[...], 0)
    for k in range(rows // LANES):
        row_lse[pl.ds(k * LANES, LANES), :] = jnp.broadcast_to(lse[k : k + 1], (LANES, LANES)).T

    parts = cols_ref[...]
    other = top_ref[...] * LOG2E
    top = jnp.maximum(jnp.max(parts, axis=0), other)
    tot = jnp.sum(jnp.exp2(parts - top[None]), axis=0) + tot_ref[...] * jnp.exp2(other - top)
    col_lse[...] = top + jnp.log2(tot) - shift_up

    def copy(y):
        return pltpu.make_async_copy(held.at[y], out_ref.at[:, pl.ds(y * width, width)], sems.at[y])

    homes = [home(shift) for shift in shifts]
    per = WIDTH // n
    for i, y in enumerate(Y_ORDER):
        for p in range(0, nx, per):
            b = jnp.concatenate([ref[i] for ref in b_refs[p : p + per]], axis=0)
            s = scores(a_ref[...], b, 2.0 * scale)
            for k in range(per):
                x = homes[p + k]
                part = s[:, k * n : (k + 1) * n]
                col = col_lse[pl.ds(y * nx + x, 1), :]
                e = jnp.exp2((part - row_lse[...]) - col)
                held[y, :, pl.ds(pl.multiple_of(x * n, n), n)] = e.astype(held.dtype)
        copy(y).start()
    for y in range(blocks):
        copy(y).wait()


def finish(a, parts, row_parts, col_parts, col_max_other, col_sum_other, shifts, scale, shift_up):
    rows = a.shape[0]
    blocks, n, _ = parts[0].shape
    width = n * len(parts)
    vmem = pl.BlockSpec(memory_space=pltpu.VMEM)
    return pl.pallas_call(
        functools.partial(finish_kernel, scale, shift_up, shifts),
        out_shape=jax.ShapeDtypeStruct((rows, blocks * width), jnp.bfloat16),
        in_specs=[vmem] * (5 + len(parts)),
        out_specs=pl.BlockSpec(memory_space=pl.ANY),
        scratch_shapes=[
            pltpu.VMEM((rows, LANES), jnp.float32),
            pltpu.VMEM((blocks * len(parts), LANES), jnp.float32),
            pltpu.VMEM((blocks, rows, width), jnp.bfloat16),
            pltpu.SemaphoreType.DMA((blocks,)),
        ],
        compiler_params=pltpu.CompilerParams(vmem_limit_bytes=VMEM_LIMIT),
        name="confidence",
    )(a, *parts, row_parts, col_parts, col_max_other.reshape(-1, LANES), col_sum_other.reshape(-1, LANES))


def shifted(block, shift):
    n = lax.axis_size("x")
    return lax.ppermute(block, "x", [(i, (i + shift) % n) for i in range(n)])


def local(feat_a, feat_b, col_max_other, col_sum_other):
    scale = LOG2E / (feat_a.shape[1] * TEMPER)
    columns = feat_b.shape[0] * lax.axis_size(AA)
    shift_up = math.log2(float(FRAME_A) * float(columns * lax.axis_size(BA)))
    shifts = (0, 2, 1, 3)
    own = spread(feat_b, "y", Y_ORDER)
    feat_a, own = lax.optimization_barrier((feat_a, own))
    a = spread(feat_a, BA).reshape(-1, feat_a.shape[1])
    parts = [own] + [shifted(own, k) for k in shifts[1:]]
    early = [early_statistics(a, parts[:2], scale)]
    row_lse, col_copies = last_statistics(a, parts[2:], early, shifts, scale, lax.axis_size(AA))
    row_parts = lax.all_gather(row_lse, BA, axis=0)
    col_parts = lax.all_to_all(col_copies, AA[::-1], 0, 0, tiled=True)
    return finish(a, parts, row_parts, col_parts, col_max_other, col_sum_other, shifts, scale, shift_up)


def solution(mesh):
    inner = Mesh(mesh.devices.reshape(8, 4, 8, 2), AA + BA)
    in_specs = (P(AA + BA, None), P(BA + AA, None), P(BA), P(BA))
    out_specs = P(AA, BA)
    return jax.shard_map(local, mesh=inner, in_specs=in_specs, out_specs=out_specs, check_vma=False)
```
